128 devices in a mesh: grp: 8 (over z, core), dev: 16 (over x, y).
Axes of the slice: x: 4, y: 4, z: 4, core: 2. Of those that a mesh axis runs over, the one named last changes fastest.
Arguments:
- probe_field: bfloat16 [896, 2, 16, 3584], P(('grp', 'dev')), may hold values from -6 to 6
- kappa_field: float32 [896, 2, 3584], P(('grp', 'dev')), may hold values from 0.5 to 2
- circle_order: int32 [896], replicated, may hold values from 0 to 895, each once
- pair_order: int32 [896], replicated, may hold values from 0 to 895, each once
- legendre_table: bfloat16 [896, 1793, 896], P(('grp', 'dev')), may hold values from -0.1875 to 0.1875
Outputs:
- filtered: bfloat16 [896, 2, 16, 3584], P(('grp', 'dev'))
The draws below stay inside these ranges and needn't reach their ends.
Inputs may be any that keep to these rules, and one draw needn't show every extreme that they name: A permutation: latitude slot s holds latitude pair circle_order[s], whose side 0 is northern circle circle_order[s] and side 1 circle 1792 - 1-circle_order[s]. A permutation: table slot s holds wavenumbers q = pair_order[s] and 1791-q.
All inputs are finite; a program needn't handle non-finite values.
Results may differ from the reference program's by a relative error of at most 0.0083.
Values may be sent and summed in bfloat16 or wider, within the bound.
No kernel may reach another device: no remote copies, remote signals or barrier semaphores. Data moves between devices by JAX's collectives and lax.ppermute only.
A program may use at most 256 MiB of HBM per device.

```python
import math
import jax
import jax.numpy as jnp
from jax import lax

NLON = 3584
PROBES = 16
LATHALF = 896
PAIRS = 896
ROWS = 1793


def block_levels(own_key, shape, cuts, least, largest):
    def one(axis_at, parts):
        draws = jax.random.uniform(jax.random.fold_in(jax.random.fold_in(own_key, 6), axis_at), (parts,), jnp.float32, least / len(cuts), largest / len(cuts))
        return jnp.repeat(jnp.exp(draws), shape[axis_at] // parts).reshape((-1,) + (1,) * (len(shape) - axis_at - 1))

    gain = one(*cuts[0])
    for cut in cuts[1:]:
        gain = gain * one(*cut)
    return gain


def normal_values(key, extent, scale, reach, pieces=(), kind=jnp.bfloat16):
    factor_of = block_levels(key, extent, pieces, -0.22, 0.18) if pieces else 1.0
    result = jax.random.normal(key, extent, jnp.float32) * scale * factor_of
    return jnp.minimum(jnp.maximum(result, -reach), reach).astype(kind)


def setup_inputs(seed: int = 0) -> dict:
    seeds = jax.random.split(jax.random.key(seed), 6)
    return {
        "probe_field": normal_values(seeds[0], (LATHALF, 2, PROBES, NLON), 1.0, 6.0, ((0, 128),)),
        "kappa_field": jnp.clip(jnp.exp(math.log(2.0) - 1.3862944 * jax.random.uniform(seeds[1], (LATHALF, 2, NLON), jnp.float32) ** block_levels(seeds[1], (LATHALF, 2, NLON), ((0, 128),), -0.2, 0.2)), 0.5, 2.0),
        "circle_order": jax.random.permutation(seeds[2], LATHALF).astype(jnp.int32),
        "pair_order": jax.random.permutation(seeds[3], PAIRS).astype(jnp.int32),
        "legendre_table": normal_values(seeds[4], (PAIRS, ROWS, LATHALF), LATHALF ** -0.5, 0.1875, ((0, 128),)),
    }


def wave_columns(pair_order, degrees):
    part_index = jnp.arange(4, dtype=jnp.int32)
    second = part_index >= 2
    wave_num = jnp.where(second[None, :], degrees - 1 - pair_order[:, None], pair_order[:, None]).reshape(-1)
    imaginary = jnp.tile(part_index % 2, pair_order.shape[0])
    return wave_num, imaginary


def forward_table(pair_order, degrees, longitudes):
    wave_num, imaginary = wave_columns(pair_order, degrees)
    phase = (jnp.arange(longitudes, dtype=jnp.int32)[:, None] * wave_num[None, :]) % longitudes
    angle = phase.astype(jnp.float32) * (2.0 * math.pi / longitudes)
    values = jnp.where(imaginary[None, :] == 1, -jnp.sin(angle), jnp.cos(angle))
    return (values * (longitudes ** -0.5)).astype(jnp.bfloat16)


def inverse_table(pair_order, degrees, longitudes):
    wave_num, imaginary = wave_columns(pair_order, degrees)
    phase = (wave_num[:, None] * jnp.arange(longitudes, dtype=jnp.int32)[None, :]) % longitudes
    angle = phase.astype(jnp.float32) * (2.0 * math.pi / longitudes)
    values = jnp.where(imaginary[:, None] == 1, -jnp.sin(angle), jnp.cos(angle))
    weight = jnp.where(wave_num == 0, 1.0, 2.0).astype(jnp.float32)
    return (values * weight[:, None] * (longitudes ** -0.5)).astype(jnp.bfloat16)


def contract_rows(left, right):
    return lax.dot_general(left, right, (((0,), (0,)), ((), ())), preferred_element_type=jnp.float32)


def legendre(table_rows, columns, pair_id):
    row_count, circle_half = table_rows.shape
    degrees = row_count - 1
    half = degrees // 2
    probes = columns.shape[1] // 8
    width = 2 * probes
    blocks = columns.reshape(circle_half, 2, 2, width)
    flip = pair_id % 2
    upper = table_rows[:half].reshape(half // 2, 2, circle_half)
    lower = table_rows[half:degrees].reshape(half // 2, 2, circle_half)
    last_row = table_rows[degrees:]
    lower_index = half + 2 * jnp.arange(half // 2, dtype=jnp.int32)
    upper_parts = []
    lower_parts = []
    lower_second = []
    for side in range(2):
        upper_parts.append(jnp.dot(upper[:, side], blocks[:, side, 0], preferred_element_type=jnp.float32))
        other = jnp.where(flip == 0, blocks[:, side, 1], blocks[:, 1 - side, 1])
        joined = jnp.concatenate([blocks[:, side, 0], other], axis=1)
        lower_prod = jnp.dot(lower[:, side], joined, preferred_element_type=jnp.float32)
        second = (lower_index + side) >= degrees - pair_id
        lower_second.append(second)
        lower_parts.append(jnp.where(second[:, None], lower_prod[:, width:], lower_prod[:, :width]))
    last_cols = jnp.where(flip == 0, blocks[:, 0, 1], blocks[:, 1, 1])
    last_prod = jnp.dot(last_row, last_cols, preferred_element_type=jnp.float32)
    spectrum = jnp.concatenate([jnp.stack(upper_parts, axis=1).reshape(half, width), jnp.stack(lower_parts, axis=1).reshape(half, width), last_prod], axis=0)
    row_index = jnp.arange(row_count, dtype=jnp.int32)
    second_all = row_index >= degrees - pair_id
    degree = jnp.where(second_all, row_index - 1, pair_id + row_index)
    degree_f = degree.astype(jnp.float32)
    damping = 1.0 / (1.0 + 4.0 * degree_f * (degree_f + 1.0) / float(degrees * degrees))
    scaled = (spectrum * damping[:, None]).astype(jnp.bfloat16)
    scaled_upper = scaled[:half].reshape(half // 2, 2, width)
    scaled_lower = scaled[half:degrees].reshape(half // 2, 2, width)
    scaled_last = scaled[degrees:]
    zero_block = jnp.zeros_like(scaled_lower[:, 0])
    first_sums = []
    second_sums = []
    for side in range(2):
        mask = lower_second[side][:, None]
        spread = jnp.concatenate([jnp.where(mask, zero_block, scaled_lower[:, side]), jnp.where(mask, scaled_lower[:, side], zero_block)], axis=1)
        lower_out = contract_rows(lower[:, side], spread)
        first_sums.append(contract_rows(upper[:, side], scaled_upper[:, side]) + lower_out[:, :width])
        second_sums.append(lower_out[:, width:])
    last_out = contract_rows(last_row, scaled_last)
    zero_out = jnp.zeros_like(last_out)
    second_even = jnp.where(flip == 0, second_sums[0], second_sums[1]) + jnp.where(flip == 0, last_out, zero_out)
    second_odd = jnp.where(flip == 0, second_sums[1], second_sums[0]) + jnp.where(flip == 0, zero_out, last_out)
    even_sum = jnp.stack([first_sums[0], second_even], axis=1)
    odd_sum = jnp.stack([first_sums[1], second_odd], axis=1)
    north_circle = (even_sum + odd_sum).reshape(circle_half, 2, 2, probes)
    south_circle = (even_sum - odd_sum).reshape(circle_half, 2, 2, probes)
    return jnp.stack([north_circle, south_circle], axis=1).astype(jnp.bfloat16)


def per_slot(bundle):
    return legendre(bundle[0], bundle[1], bundle[2])


def reference(probe_field, kappa_field, circle_order, pair_order, legendre_table):
    circle_half, hemispheres, probes, longitudes = probe_field.shape
    pair_count, row_count, circle_count = legendre_table.shape
    degrees = row_count - 1
    weighted = (kappa_field[:, :, None, :] * probe_field.astype(jnp.float32)).astype(jnp.bfloat16)
    fourier = jnp.dot(weighted.reshape(-1, longitudes), forward_table(pair_order, degrees, longitudes), preferred_element_type=jnp.float32).astype(jnp.bfloat16)
    arranged = fourier.reshape(circle_half, hemispheres, probes, pair_count, 4)
    inverse = jnp.zeros_like(circle_order).at[circle_order].set(jnp.arange(circle_half, dtype=jnp.int32))
    arranged = jnp.take(arranged, inverse, axis=0)
    north_circle = arranged[:, 0].astype(jnp.float32)
    south_circle = arranged[:, 1].astype(jnp.float32)
    halves = jnp.stack([north_circle + south_circle, north_circle - south_circle], axis=1).astype(jnp.bfloat16)
    columns = halves.transpose(3, 0, 1, 4, 2).reshape(pair_count, circle_half, 8 * probes)
    synthesis = lax.map(per_slot, (legendre_table, columns, pair_order))
    synthesis = jnp.take(synthesis, circle_order, axis=1)
    coeffs = synthesis.transpose(0, 3, 4, 1, 2, 5).reshape(4 * pair_count, circle_half * hemispheres * probes)
    values = lax.dot_general(coeffs, inverse_table(pair_order, degrees, longitudes), (((0,), (0,)), ((), ())), preferred_element_type=jnp.float32)
    return (kappa_field[:, :, None, :] * values.reshape(circle_half, hemispheres, probes, longitudes)).astype(jnp.bfloat16)
```

```python
import functools
import math

import jax
import jax.numpy as jnp
import numpy as np
from jax import lax
from jax.experimental import pallas as pl
from jax.experimental.pallas import tpu as pltpu
from jax.sharding import PartitionSpec as P

AXES = ("grp", "dev")
RADIX = 14
HALF = RADIX // 2
BLOCK = 256
WAVES = 128
NN = (((1,), (0,)), ((), ()))
NT = (((1,), (1,)), ((), ()))
TN = (((0,), (0,)), ((), ()))


def dot(left, right, dims=NN):
    return lax.dot_general(left, right, dims, preferred_element_type=jnp.float32)


@functools.lru_cache(None)
def fourier_tables(longitudes):
    degrees = longitudes // 2
    place = np.arange(BLOCK)
    wave = np.arange(WAVES)
    ahead = np.zeros((2, HALF, 2 * BLOCK, 2 * WAVES), np.float64)
    back = np.zeros((2, HALF, 2 * WAVES, 2 * BLOCK), np.float64)
    for side in range(2):
        for c in range(HALF):
            m = RADIX * wave + c
            if side:
                m = degrees - 1 - m
            angle = 2.0 * np.pi * ((m[None, :] * place[:, None]) % longitudes) / longitudes
            cos, sin = np.cos(angle), np.sin(angle)
            sign = -1.0 if side else 1.0
            ahead[side, c] = np.block([[cos, -sin], [sign * sin, sign * cos]]) * longitudes ** -0.5
            weight = np.where(m == 0, 1.0, 2.0)[:, None] * longitudes ** -0.5
            back[side, c] = np.block(
                [
                    [weight * cos.T, sign * weight * sin.T],
                    [-weight * sin.T, sign * weight * cos.T],
                ]
            )
    kind = jnp.bfloat16
    return ahead.astype(np.float32).astype(kind), back.astype(np.float32).astype(kind)


def ring(turns):
    angle = 2.0 * math.pi * (turns % RADIX) / RADIX
    return math.cos(angle), math.sin(angle)


def analyse_kernel(probe_ref, kappa_ref, table_ref, rep_ref, out_ref, y_ref, four_ref, wide_ref):
    rows = probe_ref.shape[1]
    circles = kappa_ref.shape[0]
    groups = 2 * circles

    def fold(circle, side):
        group = 2 * circle + side
        at = pl.ds(pl.multiple_of(group * rows, rows), rows)
        for lane in range(0, BLOCK, 128):
            x = []
            for b in range(RADIX):
                cut = pl.ds(b * BLOCK + lane, 128)
                scale = kappa_ref[circle, side : side + 1, cut]
                x.append(
                    (probe_ref[group, :, cut].astype(jnp.float32) * scale)
                    .astype(jnp.bfloat16)
                    .astype(jnp.float32)
                )
            s = [x[b] + x[b + HALF] for b in range(HALF)]
            d = [x[b] - x[b + HALF] for b in range(HALF)]
            even_re = [s[b] + s[HALF - b] for b in range(1, 4)]
            even_im = [s[b] - s[HALF - b] for b in range(1, 4)]
            odd_re = [d[b] - d[HALF - b] for b in range(1, 4)]
            odd_im = [d[b] + d[HALF - b] for b in range(1, 4)]
            for j in range(HALF + 1):
                first, re_terms, im_terms = (
                    (s[0], even_re, even_im) if j % 2 == 0 else (d[0], odd_re, odd_im)
                )
                real = first
                for b in range(1, 4):
                    real = real + re_terms[b - 1] * ring(j * b)[0]
                y_ref[j, at, pl.ds(lane, 128)] = real.astype(jnp.bfloat16)
                if 0 < j < HALF:
                    imag = -(im_terms[0] * ring(j)[1])
                    for b in range(2, 4):
                        imag = imag - im_terms[b - 1] * ring(j * b)[1]
                    y_ref[j, at, pl.ds(BLOCK + lane, 128)] = imag.astype(jnp.bfloat16)

    def fold_circle(circle, carry):
        fold(circle, 0)
        fold(circle, 1)
        return carry

    lax.fori_loop(0, circles, fold_circle, 0)
    for side in range(2):
        for c in range(HALF):
            j = c + side
            depth = BLOCK if j in (0, HALF) else 2 * BLOCK
            coef = dot(y_ref[j, :, :depth], table_ref[side, c, :depth, :]).astype(jnp.bfloat16)
            for group in range(groups):
                for part in range(2):
                    base = group * 4 * rows + (2 * side + part) * rows
                    four_ref[base : base + rows, c * WAVES : (c + 1) * WAVES] = coef[
                        group * rows : (group + 1) * rows, part * WAVES : (part + 1) * WAVES
                    ]
    reps = four_ref.shape[1]
    width = 8 * rows
    devices = rep_ref.shape[0] // circles
    for item in range(7):
        wide_ref[item, pl.ds(7, devices, stride=8), :] = jnp.zeros((devices, width), jnp.float32)
    lanes = lax.broadcasted_iota(jnp.int32, (devices, reps), 1)
    four = four_ref[...]
    for item in range(7):
        pick = jnp.where((rep_ref[item * devices : (item + 1) * devices, :] == lanes), 1.0, 0.0).astype(jnp.bfloat16)
        moved = dot(pick, four, NT)
        for t in range(circles):
            wide_ref[item, pl.ds(t, devices, stride=8), :] = moved[:, t * width : (t + 1) * width]
        out_ref[:, item * width : (item + 1) * width] = wide_ref[item].astype(jnp.bfloat16)


def legendre_kernel(
    pair_ref, coming_ref, table_ref, row_ref, col_ref, out_ref, x_ref, b_ref, wide_ref
):
    item = pl.program_id(0)
    items = pl.num_programs(0)
    circle_half = x_ref.shape[2]
    width = x_ref.shape[1]
    degrees = table_ref.shape[1] - 1
    half_width = width // 2

    @pl.when(item == 0)
    def _():
        slots = coming_ref.shape[0]
        where = lax.broadcasted_iota(jnp.int32, (circle_half, slots), 0)
        pick = jnp.where((row_ref[...] == where), 1.0, 0.0).astype(jnp.bfloat16)
        natural = dot(pick, coming_ref[...])
        low = lax.broadcasted_iota(jnp.int32, (circle_half, width), 1) < half_width
        for i in range(x_ref.shape[0]):
            x = natural[:, i * width : (i + 1) * width]
            other = pltpu.roll(x, half_width, 1)
            x_ref[i] = jnp.where(low, x + other, other - x).T.astype(jnp.bfloat16)

    q = pair_ref[item]
    swap = (q % RADIX >= HALF).astype(jnp.int32)

    def weights(first, count):
        row = lax.broadcasted_iota(jnp.int32, (1, count), 1) + first
        second = row >= degrees - q
        degree = jnp.where(second, row - 1, q + row).astype(jnp.float32)
        damping = 1.0 / (1.0 + 4.0 * degree * (degree + 1.0) / float(degrees * degrees))
        wave = second.astype(jnp.int32) ^ swap
        parity = jnp.where(second, row + q, row) & 1
        code = 2 * parity + wave
        return [jnp.where(code == k, damping, 0.0) for k in range(4)]

    quarter = width // 4
    spectrum = dot(x_ref[item], table_ref[0, :degrees, :], NT)
    last_row = table_ref[0, degrees:, :].astype(jnp.float32)
    last = jnp.sum(x_ref[item].astype(jnp.float32) * last_row, axis=1, keepdims=True)
    main_weights = weights(0, degrees)
    last_weights = weights(degrees, 1)
    scaled = jnp.concatenate(
        [
            (spectrum[k * quarter : (k + 1) * quarter] * main_weights[k]).astype(jnp.bfloat16)
            for k in range(4)
        ],
        axis=0,
    )
    scaled_last = jnp.concatenate(
        [
            (last[k * quarter : (k + 1) * quarter] * last_weights[k])
            .astype(jnp.bfloat16)
            .astype(jnp.float32)
            for k in range(4)
        ],
        axis=0,
    )
    total = dot(scaled, table_ref[0, :degrees, :])
    total = total + scaled_last * last_row
    even, odd = total[:half_width], total[half_width:]
    base = pl.multiple_of(item * width, width)
    b_ref[pl.ds(base, half_width), :] = (even + odd).astype(jnp.bfloat16)
    b_ref[pl.ds(base + half_width, half_width), :] = (even - odd).astype(jnp.bfloat16)

    @pl.when(item == items - 1)
    def _():
        devices = wide_ref.shape[1] // 8
        circles = col_ref.shape[0] // devices
        for t in range(circles):
            wide_ref[t, pl.ds(7, devices, stride=8), :] = jnp.zeros((devices, width), jnp.float32)
        lanes = lax.broadcasted_iota(jnp.int32, (devices, circle_half), 1)
        back = b_ref[...]
        for t in range(circles):
            pick = jnp.where((col_ref[t * devices : (t + 1) * devices, :] == lanes), 1.0, 0.0).astype(jnp.bfloat16)
            moved = dot(pick, back, NT)
            for i in range(7):
                wide_ref[t, pl.ds(i, devices, stride=8), :] = moved[:, i * width : (i + 1) * width]
            out_ref[:, t * width : (t + 1) * width] = wide_ref[t].astype(jnp.bfloat16)


def synthesise_kernel(coming_ref, kappa_ref, table_ref, rep_ref, out_ref, left_ref, u_ref):
    rows = out_ref.shape[1]
    circles = kappa_ref.shape[0]
    groups = 2 * circles
    width = 8 * rows
    slots = coming_ref.shape[0]
    reps = HALF * WAVES
    lanes = lax.broadcasted_iota(jnp.int32, (slots, reps), 1)
    pick = jnp.where((rep_ref[...] == lanes), 1.0, 0.0).astype(jnp.bfloat16)
    for t in range(circles):
        coef = dot(coming_ref[:, t * width : (t + 1) * width], pick, TN).astype(jnp.bfloat16)
        for side in range(2):
            group = 2 * t + side
            for part in range(4):
                base = side * 4 * rows + part * rows
                for c in range(HALF):
                    left_ref[
                        c + part // 2,
                        group * rows : (group + 1) * rows,
                        part * WAVES : (part + 1) * WAVES,
                    ] = coef[base : base + rows, c * WAVES : (c + 1) * WAVES]
    two = 2 * WAVES
    for j in range(HALF + 1):
        if j == 0:
            u_ref[j, :, :BLOCK] = dot(left_ref[j, :, :two], table_ref[0, 0, :, :BLOCK])
        elif j == HALF:
            u_ref[j, :, :BLOCK] = dot(left_ref[j, :, two:], table_ref[1, j - 1, :, :BLOCK])
        else:
            u_ref[j] = dot(left_ref[j, :, :two], table_ref[0, j]) + dot(
                left_ref[j, :, two:], table_ref[1, j - 1]
            )

    def unfold(circle, side):
        group = 2 * circle + side
        at = pl.ds(pl.multiple_of(group * rows, rows), rows)
        for lane in range(0, BLOCK, 128):
            real = [u_ref[j, at, pl.ds(lane, 128)] for j in range(HALF + 1)]
            imag = [None] + [u_ref[j, at, pl.ds(BLOCK + lane, 128)] for j in range(1, HALF)]
            value = [None] * RADIX
            for b in range(4):
                cos_even = real[0]
                for j in (2, 4, 6):
                    cos_even = cos_even + real[j] * ring(j * b)[0]
                cos_odd = real[HALF] * ring(HALF * b)[0]
                for j in (1, 3, 5):
                    cos_odd = cos_odd + real[j] * ring(j * b)[0]
                if b == 0:
                    value[0] = cos_even + cos_odd
                    value[HALF] = cos_even - cos_odd
                    continue
                sin_even = imag[2] * ring(2 * b)[1]
                for j in (4, 6):
                    sin_even = sin_even + imag[j] * ring(j * b)[1]
                sin_odd = imag[1] * ring(b)[1]
                for j in (3, 5):
                    sin_odd = sin_odd + imag[j] * ring(j * b)[1]
                up, down = cos_even + cos_odd, cos_even - cos_odd
                sup, sdown = sin_even + sin_odd, sin_even - sin_odd
                value[b] = up - sup
                value[RADIX - b] = up + sup
                value[HALF + b] = down - sdown
                value[HALF - b] = down + sdown
            for b in range(RADIX):
                cut = pl.ds(b * BLOCK + lane, 128)
                scale = kappa_ref[circle, side : side + 1, cut]
                out_ref[group, :, cut] = (value[b] * scale).astype(jnp.bfloat16)

    def unfold_circle(circle, carry):
        unfold(circle, 0)
        unfold(circle, 1)
        return carry

    lax.fori_loop(0, circles, unfold_circle, 0)


LIMIT = pltpu.CompilerParams(vmem_limit_bytes=56 * 2**20)
VMEM = pl.BlockSpec(memory_space=pltpu.VMEM)


def per_device(probe_field, kappa_field, circle_order, pair_order, legendre_table):
    circles, sides, probes, longitudes = probe_field.shape
    items, row_count, circle_half = legendre_table.shape
    devices = lax.axis_size(AXES)
    groups = circles * sides
    reps = HALF * WAVES
    width = 8 * probes
    ahead, back = fourier_tables(longitudes)
    ahead, back = jnp.asarray(ahead), jnp.asarray(back)

    kind, step = pair_order % RADIX, pair_order // RADIX
    rep = jnp.where(
        kind < HALF, kind * WAVES + step, (RADIX - 1 - kind) * WAVES + (WAVES - 1 - step)
    ).reshape(devices, items)
    rep_by_item = rep.T.reshape(-1, 1)
    rep_by_device = jnp.pad(rep, ((0, 0), (0, 8 - items)), constant_values=-1).reshape(-1, 1)
    circle = circle_order.reshape(devices, circles)
    circle_row = jnp.pad(circle, ((0, 0), (0, 8 - circles)), constant_values=-1).reshape(1, -1)
    circle_col = circle.T.reshape(-1, 1)
    pairs = lax.dynamic_slice(pair_order, (lax.axis_index(AXES) * items,), (items,))

    bf16, f32 = jnp.bfloat16, jnp.float32
    sending = pl.pallas_call(
        analyse_kernel,
        out_shape=jax.ShapeDtypeStruct((devices * 8, items * width), bf16),
        in_specs=[VMEM] * 4,
        out_specs=VMEM,
        scratch_shapes=[
            pltpu.VMEM((HALF + 1, groups * probes, 2 * BLOCK), bf16),
            pltpu.VMEM((circles * width, reps), bf16),
            pltpu.VMEM((items, devices * 8, width), f32),
        ],
        compiler_params=LIMIT,
        name="analyse",
    )(probe_field.reshape(groups, probes, longitudes), kappa_field, ahead, rep_by_item)

    coming = lax.all_to_all(
        sending.reshape(devices, 8, items * width), AXES, split_axis=0, concat_axis=0, tiled=True
    ).reshape(devices * 8, items * width)

    sending = pl.pallas_call(
        legendre_kernel,
        out_shape=jax.ShapeDtypeStruct((devices * 8, circles * width), bf16),
        grid_spec=pltpu.PrefetchScalarGridSpec(
            num_scalar_prefetch=1,
            grid=(items,),
            in_specs=[
                VMEM,
                pl.BlockSpec((1, row_count, circle_half), lambda i, s: (i, 0, 0)),
                VMEM,
                VMEM,
            ],
            out_specs=VMEM,
            scratch_shapes=[
                pltpu.VMEM((items, width, circle_half), bf16),
                pltpu.VMEM((items * width, circle_half), bf16),
                pltpu.VMEM((circles, devices * 8, width), f32),
            ],
        ),
        compiler_params=LIMIT,
        name="legendre",
    )(pairs, coming, legendre_table, circle_row, circle_col)

    coming = lax.all_to_all(
        sending.reshape(devices, 8, circles * width), AXES, split_axis=0, concat_axis=0, tiled=True
    ).reshape(devices * 8, circles * width)

    filtered = pl.pallas_call(
        synthesise_kernel,
        out_shape=jax.ShapeDtypeStruct((groups, probes, longitudes), bf16),
        in_specs=[VMEM] * 4,
        out_specs=VMEM,
        scratch_shapes=[
            pltpu.VMEM((HALF + 1, groups * probes, 4 * WAVES), bf16),
            pltpu.VMEM((HALF + 1, groups * probes, 2 * BLOCK), f32),
        ],
        compiler_params=LIMIT,
        name="synthesise",
    )(coming, kappa_field, back, rep_by_device)
    return filtered.reshape(circles, sides, probes, longitudes)


def solution(mesh):
    return jax.shard_map(
        per_device,
        mesh=mesh,
        in_specs=(
            P(AXES, None, None, None),
            P(AXES, None, None),
            P(),
            P(),
            P(AXES, None, None),
        ),
        out_specs=P(AXES, None, None, None),
        check_vma=False,
    )
```

```python
import functools
import math

import jax
import jax.numpy as jnp
import numpy as np
from jax import lax
from jax.experimental import pallas as pl
from jax.experimental.pallas import tpu as pltpu
from jax.sharding import PartitionSpec as P

AXES = ("grp", "dev")
RADIX = 14
HALF = RADIX // 2
BLOCK = 256
WAVES = 128
NN = (((1,), (0,)), ((), ()))
NT = (((1,), (1,)), ((), ()))
TN = (((0,), (0,)), ((), ()))


def dot(left, right, dims=NN):
    return lax.dot_general(left, right, dims, preferred_element_type=jnp.float32)


@functools.lru_cache(None)
def fourier_tables(longitudes):
    degrees = longitudes // 2
    place = np.arange(BLOCK)
    wave = np.arange(WAVES)
    ahead = np.zeros((2, HALF, 2 * BLOCK, 2 * WAVES), np.float64)
    back = np.zeros((2, HALF, 2 * WAVES, 2 * BLOCK), np.float64)
    for side in range(2):
        for c in range(HALF):
            m = RADIX * wave + c
            if side:
                m = degrees - 1 - m
            angle = 2.0 * np.pi * ((m[None, :] * place[:, None]) % longitudes) / longitudes
            cos, sin = np.cos(angle), np.sin(angle)
            sign = -1.0 if side else 1.0
            ahead[side, c] = np.block([[cos, -sin], [sign * sin, sign * cos]]) * longitudes ** -0.5
            weight = np.where(m == 0, 1.0, 2.0)[:, None] * longitudes ** -0.5
            back[side, c] = np.block(
                [
                    [weight * cos.T, sign * weight * sin.T],
                    [-weight * sin.T, sign * weight * cos.T],
                ]
            )
    kind = jnp.bfloat16
    return ahead.astype(np.float32).astype(kind), back.astype(np.float32).astype(kind)


def ring(turns):
    angle = 2.0 * math.pi * (turns % RADIX) / RADIX
    return math.cos(angle), math.sin(angle)


def representative(pairs):
    step = jnp.floor((pairs + 0.5) * (1.0 / RADIX))
    kind = pairs - RADIX * step
    other = (RADIX - 1 - kind) * WAVES + (WAVES - 1 - step)
    return jnp.where(kind < HALF, kind * WAVES + step, other)


def column(row):
    return jnp.broadcast_to(row, (row.shape[1], row.shape[1])).T


def mark_rows(pick_ref, row):
    count = pick_ref.shape[1]
    lanes = lax.broadcasted_iota(jnp.int32, (128, 128), 1).astype(jnp.float32)
    for first in range(0, row.shape[1], 128):
        upright = column(row[:, first : first + 128])
        for start in range(0, count, 128):
            hit = jnp.where(upright == lanes + float(start), 1.0, 0.0)
            pick_ref[first : first + 128, start : start + 128] = hit.astype(jnp.bfloat16)


def analyse_kernel(
    probe_hbm,
    kappa_hbm,
    table_hbm,
    pair_ref,
    out_hbm,
    probe_ref,
    kappa_ref,
    table_ref,
    y_ref,
    four_ref,
    pick_ref,
    wide_ref,
    send_ref,
    probe_sem,
    kappa_sem,
    table_sem,
    out_sem,
):
    rows = probe_ref.shape[1]
    circles = kappa_ref.shape[0]
    groups = 2 * circles
    reps = four_ref.shape[1]
    width = 8 * rows
    devices = wide_ref.shape[1] // 8

    def probe_copy(circle):
        at = pl.ds(2 * circle, 2)
        return pltpu.make_async_copy(probe_hbm.at[at], probe_ref.at[at], probe_sem.at[circle])

    kappa_copy = pltpu.make_async_copy(kappa_hbm, kappa_ref, kappa_sem)
    kappa_copy.start()
    for t in range(circles):
        probe_copy(t).start()
    table_copy = pltpu.make_async_copy(table_hbm, table_ref, table_sem)
    mark_rows(pick_ref, representative(pair_ref[...].astype(jnp.float32)))
    for t in range(circles):
        wide_ref[t, pl.ds(7, devices, stride=8), :] = jnp.zeros((devices, width), jnp.float32)
    kappa_copy.wait()

    def fold(circle, side):
        group = 2 * circle + side
        at = pl.ds(pl.multiple_of(group * rows, rows), rows)
        for lane in range(0, BLOCK, 128):
            x = []
            for b in range(RADIX):
                cut = pl.ds(b * BLOCK + lane, 128)
                scale = kappa_ref[circle, side : side + 1, cut]
                x.append(
                    (probe_ref[group, :, cut].astype(jnp.float32) * scale)
                    .astype(jnp.bfloat16)
                    .astype(jnp.float32)
                )
            s = [x[b] + x[b + HALF] for b in range(HALF)]
            d = [x[b] - x[b + HALF] for b in range(HALF)]
            even_re = [s[b] + s[HALF - b] for b in range(1, 4)]
            even_im = [s[b] - s[HALF - b] for b in range(1, 4)]
            odd_re = [d[b] - d[HALF - b] for b in range(1, 4)]
            odd_im = [d[b] + d[HALF - b] for b in range(1, 4)]
            for j in range(HALF + 1):
                first, re_terms, im_terms = (
                    (s[0], even_re, even_im) if j % 2 == 0 else (d[0], odd_re, odd_im)
                )
                real = first
                for b in range(1, 4):
                    real = real + re_terms[b - 1] * ring(j * b)[0]
                y_ref[j, at, pl.ds(lane, 128)] = real.astype(jnp.bfloat16)
                if 0 < j < HALF:
                    imag = -(im_terms[0] * ring(j)[1])
                    for b in range(2, 4):
                        imag = imag - im_terms[b - 1] * ring(j * b)[1]
                    y_ref[j, at, pl.ds(BLOCK + lane, 128)] = imag.astype(jnp.bfloat16)

    def fold_circle(circle, carry):
        probe_copy(circle).wait()

        @pl.when(circle == 1)
        def _():
            table_copy.start()

        fold(circle, 0)
        fold(circle, 1)
        return carry

    lax.fori_loop(0, circles, fold_circle, 0)
    table_copy.wait()
    for side in range(2):
        for c in range(HALF):
            j = c + side
            depth = BLOCK if j in (0, HALF) else 2 * BLOCK
            coef = dot(y_ref[j, :, :depth], table_ref[side, c, :depth, :]).astype(jnp.bfloat16)
            for group in range(groups):
                for part in range(2):
                    base = group * 4 * rows + (2 * side + part) * rows
                    four_ref[base : base + rows, c * WAVES : (c + 1) * WAVES] = coef[
                        group * rows : (group + 1) * rows, part * WAVES : (part + 1) * WAVES
                    ]
    items = wide_ref.shape[0]
    for first in range(0, circles, 2):
        last = min(first + 2, circles)
        moved = dot(pick_ref[...], four_ref[first * width : last * width, :], NT)
        for t in range(first, last):
            for item in range(items):
                wide_ref[item, pl.ds(t, devices, stride=8), :] = moved[
                    item * devices : (item + 1) * devices,
                    (t - first) * width : (t - first + 1) * width,
                ]
    copies = []
    for item in range(items):
        send_ref[item] = wide_ref[item].astype(jnp.bfloat16)
        copy = pltpu.make_async_copy(
            send_ref.at[item], out_hbm.at[:, pl.ds(item * width, width)], out_sem.at[item]
        )
        copy.start()
        copies.append(copy)
    for copy in copies:
        copy.wait()


def legendre_kernel(
    pair_ref,
    coming_ref,
    table_hbm,
    row_ref,
    order_ref,
    out_hbm,
    table_ref,
    x_ref,
    b_ref,
    pick_ref,
    back_ref,
    wide_ref,
    send_ref,
    table_sem,
    out_sem,
):
    items, width, circle_half = x_ref.shape
    degrees = table_ref.shape[1] - 1
    half_width = width // 2
    quarter = width // 4
    slots = coming_ref.shape[0]
    devices = slots // 8
    circles = wide_ref.shape[0]

    spans = [(first, min(first + 2, items)) for first in range(0, items, 2)]


    def table_copy(i):
        return pltpu.make_async_copy(table_hbm.at[i], table_ref.at[i], table_sem.at[i])

    for i in range(3):
        table_copy(i).start()
    where = lax.broadcasted_iota(jnp.int32, (circle_half, slots), 0)
    pick_ref[...] = jnp.where(row_ref[...] == where, 1.0, 0.0).astype(jnp.bfloat16)
    for first, last in spans:
        natural = dot(pick_ref[...], coming_ref[:, first * width : last * width])
        for i in range(first, last):
            x = natural[:, (i - first) * width : (i - first + 1) * width].astype(jnp.bfloat16).T
            north, south = x[:half_width].astype(jnp.float32), x[half_width:].astype(jnp.float32)
            x_ref[i, :half_width] = (north + south).astype(jnp.bfloat16)
            x_ref[i, half_width:] = (north - south).astype(jnp.bfloat16)
    mark_rows(back_ref, order_ref[...].astype(jnp.float32))
    for t in range(circles):
        wide_ref[t, pl.ds(7, devices, stride=8), :] = jnp.zeros((devices, width), jnp.float32)

    for i in range(items):
        q = pair_ref[i]
        swap = (q % RADIX >= HALF).astype(jnp.int32)

        def weights(first, length):
            row = lax.broadcasted_iota(jnp.int32, (1, length), 1) + first
            second = row >= degrees - q
            degree = jnp.where(second, row - 1, q + row).astype(jnp.float32)
            damping = 1.0 / (1.0 + 4.0 * degree * (degree + 1.0) / float(degrees * degrees))
            wave = second.astype(jnp.int32) ^ swap
            parity = jnp.where(second, row + q, row) & 1
            code = 2 * parity + wave
            return [jnp.where(code == k, damping, 0.0) for k in range(4)]

        main_weights = weights(0, degrees)
        last_weights = weights(degrees, 1)
        table_copy(i).wait()
        if i + 3 < items:
            table_copy(i + 3).start()
        spectrum = dot(x_ref[i], table_ref[i, :degrees, :], NT)
        last_row = table_ref[i, degrees:, :].astype(jnp.float32)
        last = jnp.sum(x_ref[i].astype(jnp.float32) * last_row, axis=1, keepdims=True)
        scaled = jnp.concatenate(
            [
                (spectrum[k * quarter : (k + 1) * quarter] * main_weights[k]).astype(jnp.bfloat16)
                for k in range(4)
            ],
            axis=0,
        )
        scaled_last = jnp.concatenate(
            [
                (last[k * quarter : (k + 1) * quarter] * last_weights[k])
                .astype(jnp.bfloat16)
                .astype(jnp.float32)
                for k in range(4)
            ],
            axis=0,
        )
        total = dot(scaled, table_ref[i, :degrees, :])
        total = total + scaled_last * last_row
        even, odd = total[:half_width], total[half_width:]
        b_ref[i * width : i * width + half_width, :] = (even + odd).astype(jnp.bfloat16)
        b_ref[i * width + half_width : (i + 1) * width, :] = (even - odd).astype(jnp.bfloat16)

    for first, last in spans:
        moved = dot(back_ref[...], b_ref[first * width : last * width, :], NT)
        for i in range(first, last):
            for t in range(circles):
                wide_ref[t, pl.ds(i, devices, stride=8), :] = moved[
                    t * devices : (t + 1) * devices, (i - first) * width : (i - first + 1) * width
                ]
    copies = []
    for t in range(circles):
        send_ref[t] = wide_ref[t].astype(jnp.bfloat16)
        copy = pltpu.make_async_copy(
            send_ref.at[t], out_hbm.at[:, pl.ds(t * width, width)], out_sem.at[t]
        )
        copy.start()
        copies.append(copy)
    for copy in copies:
        copy.wait()


def synthesise_kernel(
    coming_ref,
    kappa_hbm,
    table_hbm,
    pair_ref,
    out_hbm,
    kappa_ref,
    table_ref,
    pick_ref,
    turned_ref,
    left_ref,
    u_ref,
    filt_ref,
    kappa_sem,
    table_sem,
    out_sem,
):
    rows = filt_ref.shape[1]
    circles = kappa_ref.shape[0]
    width = 8 * rows
    reps = pick_ref.shape[1]

    kappa_copy = pltpu.make_async_copy(kappa_hbm, kappa_ref, kappa_sem)
    kappa_copy.start()
    table_copy = pltpu.make_async_copy(table_hbm, table_ref, table_sem)
    table_copy.start()
    mark_rows(pick_ref, representative(pair_ref[...].astype(jnp.float32)))
    for t in range(circles):
        turned_ref[t * width : (t + 1) * width, :] = coming_ref[:, t * width : (t + 1) * width].T
    for first in range(0, HALF, 2):
        last = min(first + 2, HALF)
        coef = dot(turned_ref[...], pick_ref[:, first * WAVES : last * WAVES]).astype(jnp.bfloat16)
        for t in range(circles):
            for side in range(2):
                group = 2 * t + side
                for part in range(4):
                    base = t * width + side * 4 * rows + part * rows
                    for c in range(first, last):
                        left_ref[
                            c + part // 2,
                            group * rows : (group + 1) * rows,
                            part * WAVES : (part + 1) * WAVES,
                        ] = coef[base : base + rows, (c - first) * WAVES : (c - first + 1) * WAVES]
    table_copy.wait()
    two = 2 * WAVES
    for j in range(HALF + 1):
        if j == 0:
            u_ref[j, :, :BLOCK] = dot(left_ref[j, :, :two], table_ref[0, 0, :, :BLOCK])
        elif j == HALF:
            u_ref[j, :, :BLOCK] = dot(left_ref[j, :, two:], table_ref[1, j - 1, :, :BLOCK])
        else:
            u_ref[j] = dot(left_ref[j, :, :two], table_ref[0, j]) + dot(
                left_ref[j, :, two:], table_ref[1, j - 1]
            )
    kappa_copy.wait()

    def unfold(circle, side):
        group = 2 * circle + side
        at = pl.ds(pl.multiple_of(group * rows, rows), rows)
        for lane in range(0, BLOCK, 128):
            real = [u_ref[j, at, pl.ds(lane, 128)] for j in range(HALF + 1)]
            imag = [None] + [u_ref[j, at, pl.ds(BLOCK + lane, 128)] for j in range(1, HALF)]
            value = [None] * RADIX
            for b in range(4):
                cos_even = real[0]
                for j in (2, 4, 6):
                    cos_even = cos_even + real[j] * ring(j * b)[0]
                cos_odd = real[HALF] * ring(HALF * b)[0]
                for j in (1, 3, 5):
                    cos_odd = cos_odd + real[j] * ring(j * b)[0]
                if b == 0:
                    value[0] = cos_even + cos_odd
                    value[HALF] = cos_even - cos_odd
                    continue
                sin_even = imag[2] * ring(2 * b)[1]
                for j in (4, 6):
                    sin_even = sin_even + imag[j] * ring(j * b)[1]
                sin_odd = imag[1] * ring(b)[1]
                for j in (3, 5):
                    sin_odd = sin_odd + imag[j] * ring(j * b)[1]
                up, down = cos_even + cos_odd, cos_even - cos_odd
                sup, sdown = sin_even + sin_odd, sin_even - sin_odd
                value[b] = up - sup
                value[RADIX - b] = up + sup
                value[HALF + b] = down - sdown
                value[HALF - b] = down + sdown
            for b in range(RADIX):
                cut = pl.ds(b * BLOCK + lane, 128)
                scale = kappa_ref[circle, side : side + 1, cut]
                filt_ref[group, :, cut] = (value[b] * scale).astype(jnp.bfloat16)

    def out_copy(circle):
        return pltpu.make_async_copy(
            filt_ref.at[pl.ds(2 * circle, 2)], out_hbm.at[pl.ds(2 * circle, 2)], out_sem.at[circle]
        )

    def unfold_circle(circle, carry):
        unfold(circle, 0)
        unfold(circle, 1)
        out_copy(circle).start()
        return carry

    lax.fori_loop(0, circles, unfold_circle, 0)
    for t in range(circles):
        out_copy(t).wait()


VMEM = pl.BlockSpec(memory_space=pltpu.VMEM)
SMEM = pl.BlockSpec(memory_space=pltpu.SMEM)
ANY = pl.BlockSpec(memory_space=pl.ANY)
HBM = pl.BlockSpec(memory_space=pltpu.HBM)
NOWHERE = 10000


def stay(array):
    return pltpu.with_memory_space_constraint(array, pltpu.HBM)


def near(array):
    return pltpu.with_memory_space_constraint(array, pltpu.VMEM)


def limit(mib):
    return pltpu.CompilerParams(vmem_limit_bytes=mib * 2**20)


def per_device(probe_field, kappa_field, circle_order, pair_order, legendre_table):
    circles, sides, probes, longitudes = probe_field.shape
    items, row_count, circle_half = legendre_table.shape
    devices = lax.axis_size(AXES)
    groups = circles * sides
    reps = HALF * WAVES
    width = 8 * probes
    slots = devices * 8
    ahead, back = fourier_tables(longitudes)
    ahead, back = jnp.asarray(ahead), jnp.asarray(back)

    def by_device(order, count):
        held = order.reshape(devices, count)
        return jnp.pad(held, ((0, 0), (0, 8 - count)), constant_values=NOWHERE).reshape(1, slots)

    def by_place(order, count):
        return order.reshape(devices, count).T.reshape(1, count * devices)

    def swap_over(payload):
        blocks = payload.reshape(devices, 8, payload.shape[1])
        moved = lax.all_to_all(blocks, AXES, split_axis=0, concat_axis=0, tiled=True)
        return moved.reshape(payload.shape)

    bf16, f32 = jnp.bfloat16, jnp.float32
    dma = pltpu.SemaphoreType.DMA
    sending = pl.pallas_call(
        analyse_kernel,
        out_shape=pltpu.HBM((slots, items * width), bf16),
        in_specs=[HBM, HBM, HBM, VMEM],
        out_specs=HBM,
        scratch_shapes=[
            pltpu.VMEM((groups, probes, longitudes), bf16),
            pltpu.VMEM(kappa_field.shape, f32),
            pltpu.VMEM(ahead.shape, bf16),
            pltpu.VMEM((HALF + 1, groups * probes, 2 * BLOCK), bf16),
            pltpu.VMEM((circles * width, reps), bf16),
            pltpu.VMEM((items * devices, reps), bf16),
            pltpu.VMEM((items, slots, width), f32),
            pltpu.VMEM((items, slots, width), bf16),
            dma((circles,)),
            dma,
            dma,
            dma((items,)),
        ],
        compiler_params=limit(40),
        name="analyse",
    )(
        stay(probe_field.reshape(groups, probes, longitudes)),
        stay(kappa_field),
        stay(ahead),
        by_place(pair_order, items),
    )
    coming = swap_over(sending)

    pairs = lax.dynamic_slice(pair_order, (lax.axis_index(AXES) * items,), (items,))
    sending = pl.pallas_call(
        legendre_kernel,
        out_shape=pltpu.HBM((slots, circles * width), bf16),
        in_specs=[SMEM, VMEM, HBM, VMEM, VMEM],
        out_specs=HBM,
        scratch_shapes=[
            pltpu.VMEM((items, row_count, circle_half), bf16),
            pltpu.VMEM((items, width, circle_half), bf16),
            pltpu.VMEM((items * width, circle_half), bf16),
            pltpu.VMEM((circle_half, slots), bf16),
            pltpu.VMEM((circles * devices, circle_half), bf16),
            pltpu.VMEM((circles, slots, width), f32),
            pltpu.VMEM((circles, slots, width), bf16),
            dma((items,)),
            dma((circles,)),
        ],
        compiler_params=limit(48),
        name="legendre",
    )(
        pairs,
        near(coming),
        stay(legendre_table),
        by_device(circle_order, circles),
        by_place(circle_order, circles),
    )
    coming = swap_over(sending)

    filtered = pl.pallas_call(
        synthesise_kernel,
        out_shape=jax.ShapeDtypeStruct((groups, probes, longitudes), bf16),
        in_specs=[VMEM, HBM, HBM, VMEM],
        out_specs=HBM,
        scratch_shapes=[
            pltpu.VMEM(kappa_field.shape, f32),
            pltpu.VMEM(back.shape, bf16),
            pltpu.VMEM((slots, reps), bf16),
            pltpu.VMEM((circles * width, slots), bf16),
            pltpu.VMEM((HALF + 1, groups * probes, 4 * WAVES), bf16),
            pltpu.VMEM((HALF + 1, groups * probes, 2 * BLOCK), f32),
            pltpu.VMEM((groups, probes, longitudes), bf16),
            dma,
            dma,
            dma((circles,)),
        ],
        compiler_params=limit(40),
        name="synthesise",
    )(
        near(coming), stay(kappa_field), stay(back), by_device(pair_order, items)
    )
    return filtered.reshape(circles, sides, probes, longitudes)


def solution(mesh):
    return jax.shard_map(
        per_device,
        mesh=mesh,
        in_specs=(
            P(AXES, None, None, None),
            P(AXES, None, None),
            P(),
            P(),
            P(AXES, None, None),
        ),
        out_specs=P(AXES, None, None, None),
        check_vma=False,
    )
```

```python
import functools
import math

import jax
import jax.numpy as jnp
import numpy as np
from jax import lax
from jax.experimental import pallas as pl
from jax.experimental.pallas import tpu as pltpu
from jax.sharding import PartitionSpec as P

AXES = ("grp", "dev")
RADIX = 14
HALF = RADIX // 2
BLOCK = 256
WAVES = 128
NN = (((1,), (0,)), ((), ()))
NT = (((1,), (1,)), ((), ()))
TN = (((0,), (0,)), ((), ()))


def dot(left, right, dims=NN):
    return lax.dot_general(left, right, dims, preferred_element_type=jnp.float32)


@functools.lru_cache(None)
def fourier_tables(longitudes):
    degrees = longitudes // 2
    place = np.arange(BLOCK)
    wave = np.arange(WAVES)
    ahead = np.zeros((2, HALF, 2 * BLOCK, 2 * WAVES), np.float64)
    back = np.zeros((2, HALF, 2 * WAVES, 2 * BLOCK), np.float64)
    for side in range(2):
        for c in range(HALF):
            m = RADIX * wave + c
            if side:
                m = degrees - 1 - m
            angle = 2.0 * np.pi * ((m[None, :] * place[:, None]) % longitudes) / longitudes
            cos, sin = np.cos(angle), np.sin(angle)
            sign = -1.0 if side else 1.0
            ahead[side, c] = np.block([[cos, -sin], [sign * sin, sign * cos]]) * longitudes ** -0.5
            weight = np.where(m == 0, 1.0, 2.0)[:, None] * longitudes ** -0.5
            back[side, c] = np.block(
                [
                    [weight * cos.T, sign * weight * sin.T],
                    [-weight * sin.T, sign * weight * cos.T],
                ]
            )
    kind = jnp.bfloat16
    return ahead.astype(np.float32).astype(kind), back.astype(np.float32).astype(kind)


def ring(turns):
    angle = 2.0 * math.pi * (turns % RADIX) / RADIX
    return math.cos(angle), math.sin(angle)


def representative(pairs):
    step = jnp.floor((pairs + 0.5) * (1.0 / RADIX))
    kind = pairs - RADIX * step
    other = (RADIX - 1 - kind) * WAVES + (WAVES - 1 - step)
    return jnp.where(kind < HALF, kind * WAVES + step, other)


def column(row):
    return jnp.broadcast_to(row, (row.shape[1], row.shape[1])).T


def mark_rows(pick_ref, row):
    count = pick_ref.shape[1]
    lanes = lax.broadcasted_iota(jnp.int32, (128, 128), 1).astype(jnp.float32)
    for first in range(0, row.shape[1], 128):
        upright = column(row[:, first : first + 128])
        for start in range(0, count, 128):
            hit = jnp.where(upright == lanes + float(start), 1.0, 0.0)
            pick_ref[first : first + 128, start : start + 128] = hit.astype(jnp.bfloat16)


def analyse_kernel(
    probe_hbm,
    kappa_hbm,
    table_hbm,
    pair_ref,
    out_hbm,
    probe_ref,
    kappa_ref,
    table_ref,
    y_ref,
    four_ref,
    pick_ref,
    wide_ref,
    send_ref,
    probe_sem,
    kappa_sem,
    table_sem,
    out_sem,
):
    rows = probe_ref.shape[1]
    circles = kappa_ref.shape[0]
    groups = 2 * circles
    reps = four_ref.shape[1]
    width = 8 * rows
    devices = wide_ref.shape[1] // 8

    def probe_copy(circle):
        at = pl.ds(2 * circle, 2)
        return pltpu.make_async_copy(probe_hbm.at[at], probe_ref.at[at], probe_sem.at[circle])

    kappa_copy = pltpu.make_async_copy(kappa_hbm, kappa_ref, kappa_sem)
    kappa_copy.start()
    for t in range(circles):
        probe_copy(t).start()

    def table_copy(side):
        return pltpu.make_async_copy(table_hbm.at[side], table_ref.at[side], table_sem.at[side])

    mark_rows(pick_ref, representative(pair_ref[...].astype(jnp.float32)))
    for t in range(circles):
        wide_ref[t, pl.ds(7, devices, stride=8), :] = jnp.zeros((devices, width), jnp.float32)
    kappa_copy.wait()

    def fold(circle, side):
        group = 2 * circle + side
        at = pl.ds(pl.multiple_of(group * rows, rows), rows)
        for lane in range(0, BLOCK, 128):
            x = []
            for b in range(RADIX):
                cut = pl.ds(b * BLOCK + lane, 128)
                scale = kappa_ref[circle, side : side + 1, cut]
                x.append(
                    (probe_ref[group, :, cut].astype(jnp.float32) * scale)
                    .astype(jnp.bfloat16)
                    .astype(jnp.float32)
                )
            s = [x[b] + x[b + HALF] for b in range(HALF)]
            d = [x[b] - x[b + HALF] for b in range(HALF)]
            even_re = [s[b] + s[HALF - b] for b in range(1, 4)]
            even_im = [s[b] - s[HALF - b] for b in range(1, 4)]
            odd_re = [d[b] - d[HALF - b] for b in range(1, 4)]
            odd_im = [d[b] + d[HALF - b] for b in range(1, 4)]
            for j in range(HALF + 1):
                first, re_terms, im_terms = (
                    (s[0], even_re, even_im) if j % 2 == 0 else (d[0], odd_re, odd_im)
                )
                real = first
                for b in range(1, 4):
                    real = real + re_terms[b - 1] * ring(j * b)[0]
                y_ref[j, at, pl.ds(lane, 128)] = real.astype(jnp.bfloat16)
                if 0 < j < HALF:
                    imag = -(im_terms[0] * ring(j)[1])
                    for b in range(2, 4):
                        imag = imag - im_terms[b - 1] * ring(j * b)[1]
                    y_ref[j, at, pl.ds(BLOCK + lane, 128)] = imag.astype(jnp.bfloat16)

    def fold_circle(circle, carry):
        probe_copy(circle).wait()

        @pl.when(circle == 0)
        def _():
            table_copy(0).start()
            table_copy(1).start()

        fold(circle, 0)
        fold(circle, 1)
        return carry

    lax.fori_loop(0, circles, fold_circle, 0)
    for side in range(2):
        table_copy(side).wait()
        for c in range(HALF):
            j = c + side
            depth = BLOCK if j in (0, HALF) else 2 * BLOCK
            coef = dot(y_ref[j, :, :depth], table_ref[side, c, :depth, :]).astype(jnp.bfloat16)
            for group in range(groups):
                for part in range(2):
                    base = group * 4 * rows + (2 * side + part) * rows
                    four_ref[base : base + rows, c * WAVES : (c + 1) * WAVES] = coef[
                        group * rows : (group + 1) * rows, part * WAVES : (part + 1) * WAVES
                    ]
    items = wide_ref.shape[0]
    for first in range(0, circles, 2):
        last = min(first + 2, circles)
        moved = dot(pick_ref[...], four_ref[first * width : last * width, :], NT)
        for t in range(first, last):
            for item in range(items):
                wide_ref[item, pl.ds(t, devices, stride=8), :] = moved[
                    item * devices : (item + 1) * devices,
                    (t - first) * width : (t - first + 1) * width,
                ]
    copies = []
    for item in range(items):
        send_ref[item] = wide_ref[item].astype(jnp.bfloat16)
        copy = pltpu.make_async_copy(
            send_ref.at[item], out_hbm.at[:, pl.ds(item * width, width)], out_sem.at[item]
        )
        copy.start()
        copies.append(copy)
    for copy in copies:
        copy.wait()


def legendre_kernel(
    pair_ref,
    coming_ref,
    table_hbm,
    row_ref,
    order_ref,
    out_hbm,
    table_ref,
    x_ref,
    b_ref,
    pick_ref,
    back_ref,
    wide_ref,
    send_ref,
    table_sem,
    out_sem,
):
    items, width, circle_half = x_ref.shape
    degrees = table_ref.shape[1] - 1
    half_width = width // 2
    quarter = width // 4
    slots = coming_ref.shape[0]
    devices = slots // 8
    circles = wide_ref.shape[0]

    spans = [(first, min(first + 2, items)) for first in range(0, items, 2)]


    def table_copy(i):
        return pltpu.make_async_copy(table_hbm.at[i], table_ref.at[i], table_sem.at[i])

    for i in range(3):
        table_copy(i).start()
    where = lax.broadcasted_iota(jnp.int32, (circle_half, slots), 0)
    pick_ref[...] = jnp.where(row_ref[...] == where, 1.0, 0.0).astype(jnp.bfloat16)
    for first, last in spans:
        natural = dot(pick_ref[...], coming_ref[:, first * width : last * width])
        for i in range(first, last):
            x = natural[:, (i - first) * width : (i - first + 1) * width].astype(jnp.bfloat16).T
            north, south = x[:half_width].astype(jnp.float32), x[half_width:].astype(jnp.float32)
            x_ref[i, :half_width] = (north + south).astype(jnp.bfloat16)
            x_ref[i, half_width:] = (north - south).astype(jnp.bfloat16)
    mark_rows(back_ref, order_ref[...].astype(jnp.float32))
    for t in range(circles):
        wide_ref[t, pl.ds(7, devices, stride=8), :] = jnp.zeros((devices, width), jnp.float32)

    for i in range(items):
        q = pair_ref[i]
        swap = (q % RADIX >= HALF).astype(jnp.int32)

        def weights(first, length):
            row = lax.broadcasted_iota(jnp.int32, (1, length), 1) + first
            second = row >= degrees - q
            degree = jnp.where(second, row - 1, q + row).astype(jnp.float32)
            damping = 1.0 / (1.0 + 4.0 * degree * (degree + 1.0) / float(degrees * degrees))
            wave = second.astype(jnp.int32) ^ swap
            parity = jnp.where(second, row + q, row) & 1
            code = 2 * parity + wave
            return [jnp.where(code == k, damping, 0.0) for k in range(4)]

        main_weights = weights(0, degrees)
        last_weights = weights(degrees, 1)
        table_copy(i).wait()
        if i + 3 < items:
            table_copy(i + 3).start()
        spectrum = dot(x_ref[i], table_ref[i, :degrees, :], NT)
        last_row = table_ref[i, degrees:, :].astype(jnp.float32)
        last = jnp.sum(x_ref[i].astype(jnp.float32) * last_row, axis=1, keepdims=True)
        scaled = jnp.concatenate(
            [
                (spectrum[k * quarter : (k + 1) * quarter] * main_weights[k]).astype(jnp.bfloat16)
                for k in range(4)
            ],
            axis=0,
        )
        scaled_last = jnp.concatenate(
            [
                (last[k * quarter : (k + 1) * quarter] * last_weights[k])
                .astype(jnp.bfloat16)
                .astype(jnp.float32)
                for k in range(4)
            ],
            axis=0,
        )
        total = dot(scaled, table_ref[i, :degrees, :])
        total = total + scaled_last * last_row
        even, odd = total[:half_width], total[half_width:]
        b_ref[i * width : i * width + half_width, :] = (even + odd).astype(jnp.bfloat16)
        b_ref[i * width + half_width : (i + 1) * width, :] = (even - odd).astype(jnp.bfloat16)

    for first, last in spans:
        moved = dot(back_ref[...], b_ref[first * width : last * width, :], NT)
        for i in range(first, last):
            for t in range(circles):
                wide_ref[t, pl.ds(i, devices, stride=8), :] = moved[
                    t * devices : (t + 1) * devices, (i - first) * width : (i - first + 1) * width
                ]
    copies = []
    for t in range(circles):
        send_ref[t] = wide_ref[t].astype(jnp.bfloat16)
        copy = pltpu.make_async_copy(
            send_ref.at[t], out_hbm.at[:, pl.ds(t * width, width)], out_sem.at[t]
        )
        copy.start()
        copies.append(copy)
    for copy in copies:
        copy.wait()


def synthesise_kernel(
    coming_ref,
    kappa_hbm,
    table_hbm,
    pair_ref,
    out_hbm,
    kappa_ref,
    table_ref,
    pick_ref,
    turned_ref,
    left_ref,
    u_ref,
    filt_ref,
    kappa_sem,
    table_sem,
    out_sem,
):
    rows = filt_ref.shape[1]
    circles = kappa_ref.shape[0]
    width = 8 * rows
    reps = pick_ref.shape[1]

    kappa_copy = pltpu.make_async_copy(kappa_hbm, kappa_ref, kappa_sem)
    kappa_copy.start()
    table_copy = pltpu.make_async_copy(table_hbm, table_ref, table_sem)
    table_copy.start()
    mark_rows(pick_ref, representative(pair_ref[...].astype(jnp.float32)))
    for t in range(circles):
        turned_ref[t * width : (t + 1) * width, :] = coming_ref[:, t * width : (t + 1) * width].T
    for first in range(0, HALF, 2):
        last = min(first + 2, HALF)
        coef = dot(turned_ref[...], pick_ref[:, first * WAVES : last * WAVES]).astype(jnp.bfloat16)
        for t in range(circles):
            for side in range(2):
                group = 2 * t + side
                for part in range(4):
                    base = t * width + side * 4 * rows + part * rows
                    for c in range(first, last):
                        left_ref[
                            c + part // 2,
                            group * rows : (group + 1) * rows,
                            part * WAVES : (part + 1) * WAVES,
                        ] = coef[base : base + rows, (c - first) * WAVES : (c - first + 1) * WAVES]
    table_copy.wait()
    two = 2 * WAVES
    for j in range(HALF + 1):
        if j == 0:
            u_ref[j, :, :BLOCK] = dot(left_ref[j, :, :two], table_ref[0, 0, :, :BLOCK])
        elif j == HALF:
            u_ref[j, :, :BLOCK] = dot(left_ref[j, :, two:], table_ref[1, j - 1, :, :BLOCK])
        else:
            u_ref[j] = dot(left_ref[j, :, :two], table_ref[0, j]) + dot(
                left_ref[j, :, two:], table_ref[1, j - 1]
            )
    kappa_copy.wait()

    def unfold(circle, side):
        group = 2 * circle + side
        at = pl.ds(pl.multiple_of(group * rows, rows), rows)
        for lane in range(0, BLOCK, 128):
            real = [u_ref[j, at, pl.ds(lane, 128)] for j in range(HALF + 1)]
            imag = [None] + [u_ref[j, at, pl.ds(BLOCK + lane, 128)] for j in range(1, HALF)]
            value = [None] * RADIX
            for b in range(4):
                cos_even = real[0]
                for j in (2, 4, 6):
                    cos_even = cos_even + real[j] * ring(j * b)[0]
                cos_odd = real[HALF] * ring(HALF * b)[0]
                for j in (1, 3, 5):
                    cos_odd = cos_odd + real[j] * ring(j * b)[0]
                if b == 0:
                    value[0] = cos_even + cos_odd
                    value[HALF] = cos_even - cos_odd
                    continue
                sin_even = imag[2] * ring(2 * b)[1]
                for j in (4, 6):
                    sin_even = sin_even + imag[j] * ring(j * b)[1]
                sin_odd = imag[1] * ring(b)[1]
                for j in (3, 5):
                    sin_odd = sin_odd + imag[j] * ring(j * b)[1]
                up, down = cos_even + cos_odd, cos_even - cos_odd
                sup, sdown = sin_even + sin_odd, sin_even - sin_odd
                value[b] = up - sup
                value[RADIX - b] = up + sup
                value[HALF + b] = down - sdown
                value[HALF - b] = down + sdown
            for b in range(RADIX):
                cut = pl.ds(b * BLOCK + lane, 128)
                scale = kappa_ref[circle, side : side + 1, cut]
                filt_ref[group, :, cut] = (value[b] * scale).astype(jnp.bfloat16)

    def out_copy(circle):
        return pltpu.make_async_copy(
            filt_ref.at[pl.ds(2 * circle, 2)], out_hbm.at[pl.ds(2 * circle, 2)], out_sem.at[circle]
        )

    def unfold_circle(circle, carry):
        unfold(circle, 0)
        unfold(circle, 1)
        out_copy(circle).start()
        return carry

    lax.fori_loop(0, circles, unfold_circle, 0)
    for t in range(circles):
        out_copy(t).wait()


VMEM = pl.BlockSpec(memory_space=pltpu.VMEM)
SMEM = pl.BlockSpec(memory_space=pltpu.SMEM)
ANY = pl.BlockSpec(memory_space=pl.ANY)
HBM = pl.BlockSpec(memory_space=pltpu.HBM)
NOWHERE = 10000


def stay(array):
    return pltpu.with_memory_space_constraint(array, pltpu.HBM)


def near(array):
    return pltpu.with_memory_space_constraint(array, pltpu.VMEM)


def limit(mib):
    return pltpu.CompilerParams(vmem_limit_bytes=mib * 2**20)


def per_device(probe_field, kappa_field, circle_order, pair_order, legendre_table):
    circles, sides, probes, longitudes = probe_field.shape
    items, row_count, circle_half = legendre_table.shape
    devices = lax.axis_size(AXES)
    groups = circles * sides
    reps = HALF * WAVES
    width = 8 * probes
    slots = devices * 8
    ahead, back = fourier_tables(longitudes)
    ahead, back = jnp.asarray(ahead), jnp.asarray(back)

    def by_device(order, count):
        held = order.reshape(devices, count)
        return jnp.pad(held, ((0, 0), (0, 8 - count)), constant_values=NOWHERE).reshape(1, slots)

    def by_place(order, count):
        return order.reshape(devices, count).T.reshape(1, count * devices)

    def swap_over(payload):
        blocks = payload.reshape(devices, 8, payload.shape[1])
        moved = lax.all_to_all(blocks, AXES, split_axis=0, concat_axis=0, tiled=True)
        return moved.reshape(payload.shape)

    bf16, f32 = jnp.bfloat16, jnp.float32
    dma = pltpu.SemaphoreType.DMA
    sending = pl.pallas_call(
        analyse_kernel,
        out_shape=pltpu.HBM((slots, items * width), bf16),
        in_specs=[HBM, HBM, HBM, VMEM],
        out_specs=HBM,
        scratch_shapes=[
            pltpu.VMEM((groups, probes, longitudes), bf16),
            pltpu.VMEM(kappa_field.shape, f32),
            pltpu.VMEM(ahead.shape, bf16),
            pltpu.VMEM((HALF + 1, groups * probes, 2 * BLOCK), bf16),
            pltpu.VMEM((circles * width, reps), bf16),
            pltpu.VMEM((items * devices, reps), bf16),
            pltpu.VMEM((items, slots, width), f32),
            pltpu.VMEM((items, slots, width), bf16),
            dma((circles,)),
            dma,
            dma((2,)),
            dma((items,)),
        ],
        compiler_params=limit(40),
        name="analyse",
    )(
        stay(probe_field.reshape(groups, probes, longitudes)),
        stay(kappa_field),
        stay(ahead),
        by_place(pair_order, items),
    )
    coming = swap_over(sending)

    pairs = lax.dynamic_slice(pair_order, (lax.axis_index(AXES) * items,), (items,))
    sending = pl.pallas_call(
        legendre_kernel,
        out_shape=pltpu.HBM((slots, circles * width), bf16),
        in_specs=[SMEM, VMEM, HBM, VMEM, VMEM],
        out_specs=HBM,
        scratch_shapes=[
            pltpu.VMEM((items, row_count, circle_half), bf16),
            pltpu.VMEM((items, width, circle_half), bf16),
            pltpu.VMEM((items * width, circle_half), bf16),
            pltpu.VMEM((circle_half, slots), bf16),
            pltpu.VMEM((circles * devices, circle_half), bf16),
            pltpu.VMEM((circles, slots, width), f32),
            pltpu.VMEM((circles, slots, width), bf16),
            dma((items,)),
            dma((circles,)),
        ],
        compiler_params=limit(48),
        name="legendre",
    )(
        pairs,
        near(coming),
        stay(legendre_table),
        by_device(circle_order, circles),
        by_place(circle_order, circles),
    )
    coming = swap_over(sending)

    filtered = pl.pallas_call(
        synthesise_kernel,
        out_shape=jax.ShapeDtypeStruct((groups, probes, longitudes), bf16),
        in_specs=[VMEM, HBM, HBM, VMEM],
        out_specs=HBM,
        scratch_shapes=[
            pltpu.VMEM(kappa_field.shape, f32),
            pltpu.VMEM(back.shape, bf16),
            pltpu.VMEM((slots, reps), bf16),
            pltpu.VMEM((circles * width, slots), bf16),
            pltpu.VMEM((HALF + 1, groups * probes, 4 * WAVES), bf16),
            pltpu.VMEM((HALF + 1, groups * probes, 2 * BLOCK), f32),
            pltpu.VMEM((groups, probes, longitudes), bf16),
            dma,
            dma,
            dma((circles,)),
        ],
        compiler_params=limit(40),
        name="synthesise",
    )(
        near(coming), stay(kappa_field), stay(back), by_device(pair_order, items)
    )
    return filtered.reshape(circles, sides, probes, longitudes)


def solution(mesh):
    return jax.shard_map(
        per_device,
        mesh=mesh,
        in_specs=(
            P(AXES, None, None, None),
            P(AXES, None, None),
            P(),
            P(),
            P(AXES, None, None),
        ),
        out_specs=P(AXES, None, None, None),
        check_vma=False,
    )
```

```python
import functools
import math

import jax
import jax.numpy as jnp
import numpy as np
from jax import lax
from jax.experimental import pallas as pl
from jax.experimental.pallas import tpu as pltpu
from jax.sharding import PartitionSpec as P

AXES = ("grp", "dev")
RADIX = 14
HALF = RADIX // 2
BLOCK = 256
WAVES = 128
NN = (((1,), (0,)), ((), ()))
NT = (((1,), (1,)), ((), ()))
TN = (((0,), (0,)), ((), ()))


def dot(left, right, dims=NN):
    return lax.dot_general(left, right, dims, preferred_element_type=jnp.float32)


@functools.lru_cache(None)
def fourier_tables(longitudes):
    degrees = longitudes // 2
    place = np.arange(BLOCK)
    wave = np.arange(WAVES)
    ahead = np.zeros((2, HALF, 2 * BLOCK, 2 * WAVES), np.float64)
    back = np.zeros((2, HALF, 2 * WAVES, 2 * BLOCK), np.float64)
    for side in range(2):
        for c in range(HALF):
            m = RADIX * wave + c
            if side:
                m = degrees - 1 - m
            angle = 2.0 * np.pi * ((m[None, :] * place[:, None]) % longitudes) / longitudes
            cos, sin = np.cos(angle), np.sin(angle)
            sign = -1.0 if side else 1.0
            ahead[side, c] = np.block([[cos, -sin], [sign * sin, sign * cos]]) * longitudes ** -0.5
            weight = np.where(m == 0, 1.0, 2.0)[:, None] * longitudes ** -0.5
            back[side, c] = np.block(
                [
                    [weight * cos.T, sign * weight * sin.T],
                    [-weight * sin.T, sign * weight * cos.T],
                ]
            )
    kind = jnp.bfloat16
    return ahead.astype(np.float32).astype(kind), back.astype(np.float32).astype(kind)


def ring(turns):
    angle = 2.0 * math.pi * (turns % RADIX) / RADIX
    return math.cos(angle), math.sin(angle)


def representative(pairs):
    step = jnp.floor((pairs + 0.5) * (1.0 / RADIX))
    kind = pairs - RADIX * step
    other = (RADIX - 1 - kind) * WAVES + (WAVES - 1 - step)
    return jnp.where(kind < HALF, kind * WAVES + step, other)


def column(row):
    return jnp.broadcast_to(row, (row.shape[1], row.shape[1])).T


def mark_rows(pick_ref, row):
    count = pick_ref.shape[1]
    lanes = lax.broadcasted_iota(jnp.int32, (128, 128), 1).astype(jnp.float32)
    for first in range(0, row.shape[1], 128):
        upright = column(row[:, first : first + 128])
        for start in range(0, count, 128):
            hit = jnp.where(upright == lanes + float(start), 1.0, 0.0)
            pick_ref[first : first + 128, start : start + 128] = hit.astype(jnp.bfloat16)


def analyse_kernel(
    probe_hbm,
    kappa_hbm,
    table_hbm,
    pair_ref,
    out_hbm,
    probe_ref,
    kappa_ref,
    table_ref,
    y_ref,
    four_ref,
    pick_ref,
    wide_ref,
    send_ref,
    upright_ref,
    probe_sem,
    kappa_sem,
    table_sem,
    out_sem,
):
    rows = probe_ref.shape[1]
    circles = kappa_ref.shape[0]
    groups = 2 * circles
    reps = four_ref.shape[1]
    width = 8 * rows
    devices = wide_ref.shape[1] // 8

    def probe_copy(circle):
        at = pl.ds(2 * circle, 2)
        return pltpu.make_async_copy(probe_hbm.at[at], probe_ref.at[at], probe_sem.at[circle])

    kappa_copy = pltpu.make_async_copy(kappa_hbm, kappa_ref, kappa_sem)
    kappa_copy.start()
    for t in range(circles):
        probe_copy(t).start()

    def table_copy(side):
        return pltpu.make_async_copy(table_hbm.at[side], table_ref.at[side], table_sem.at[side])

    rep = representative(pair_ref[...].astype(jnp.float32))
    for r in range(rep.shape[0]):
        upright_ref[r * devices : (r + 1) * devices, :] = column(rep[r : r + 1])
    lanes = lax.broadcasted_iota(jnp.int32, (devices, WAVES), 1).astype(jnp.float32)
    for item in range(rep.shape[0]):
        upright = upright_ref[pl.ds(item, devices, stride=rep.shape[0]), :]
        for start in range(0, reps, WAVES):
            hit = jnp.where(upright == lanes + float(start), 1.0, 0.0)
            pick_ref[item * devices : (item + 1) * devices, start : start + WAVES] = hit.astype(
                jnp.bfloat16
            )
    for t in range(circles):
        wide_ref[t, pl.ds(7, devices, stride=8), :] = jnp.zeros((devices, width), jnp.float32)
    kappa_copy.wait()

    def fold(circle, side):
        group = 2 * circle + side
        at = pl.ds(pl.multiple_of(group * rows, rows), rows)
        for lane in range(0, BLOCK, 128):
            x = []
            for b in range(RADIX):
                cut = pl.ds(b * BLOCK + lane, 128)
                scale = kappa_ref[circle, side : side + 1, cut]
                x.append(
                    (probe_ref[group, :, cut].astype(jnp.float32) * scale)
                    .astype(jnp.bfloat16)
                    .astype(jnp.float32)
                )
            s = [x[b] + x[b + HALF] for b in range(HALF)]
            d = [x[b] - x[b + HALF] for b in range(HALF)]
            even_re = [s[b] + s[HALF - b] for b in range(1, 4)]
            even_im = [s[b] - s[HALF - b] for b in range(1, 4)]
            odd_re = [d[b] - d[HALF - b] for b in range(1, 4)]
            odd_im = [d[b] + d[HALF - b] for b in range(1, 4)]
            for j in range(HALF + 1):
                first, re_terms, im_terms = (
                    (s[0], even_re, even_im) if j % 2 == 0 else (d[0], odd_re, odd_im)
                )
                real = first
                for b in range(1, 4):
                    real = real + re_terms[b - 1] * ring(j * b)[0]
                y_ref[j, at, pl.ds(lane, 128)] = real.astype(jnp.bfloat16)
                if 0 < j < HALF:
                    imag = -(im_terms[0] * ring(j)[1])
                    for b in range(2, 4):
                        imag = imag - im_terms[b - 1] * ring(j * b)[1]
                    y_ref[j, at, pl.ds(BLOCK + lane, 128)] = imag.astype(jnp.bfloat16)

    def fold_circle(circle, carry):
        probe_copy(circle).wait()

        @pl.when(circle == 0)
        def _():
            table_copy(0).start()
            table_copy(1).start()

        fold(circle, 0)
        fold(circle, 1)
        return carry

    lax.fori_loop(0, circles, fold_circle, 0)
    for side in range(2):
        table_copy(side).wait()
        for c in range(HALF):
            j = c + side
            depth = BLOCK if j in (0, HALF) else 2 * BLOCK
            coef = dot(y_ref[j, :, :depth], table_ref[side, c, :depth, :]).astype(jnp.bfloat16)
            for group in range(groups):
                for part in range(2):
                    base = group * 4 * rows + (2 * side + part) * rows
                    four_ref[base : base + rows, c * WAVES : (c + 1) * WAVES] = coef[
                        group * rows : (group + 1) * rows, part * WAVES : (part + 1) * WAVES
                    ]
    items = wide_ref.shape[0]
    for first in range(0, circles, 2):
        last = min(first + 2, circles)
        moved = dot(pick_ref[...], four_ref[first * width : last * width, :], NT)
        for t in range(first, last):
            for item in range(items):
                wide_ref[item, pl.ds(t, devices, stride=8), :] = moved[
                    item * devices : (item + 1) * devices,
                    (t - first) * width : (t - first + 1) * width,
                ]
    copies = []
    for item in range(items):
        send_ref[item] = wide_ref[item].astype(jnp.bfloat16)
        copy = pltpu.make_async_copy(
            send_ref.at[item], out_hbm.at[:, pl.ds(item * width, width)], out_sem.at[item]
        )
        copy.start()
        copies.append(copy)
    for copy in copies:
        copy.wait()


def legendre_kernel(
    pair_ref,
    coming_ref,
    table_hbm,
    row_ref,
    order_ref,
    out_hbm,
    table_ref,
    x_ref,
    b_ref,
    pick_ref,
    back_ref,
    wide_ref,
    send_ref,
    table_sem,
    out_sem,
):
    items, width, circle_half = x_ref.shape
    degrees = table_ref.shape[1] - 1
    half_width = width // 2
    quarter = width // 4
    slots = coming_ref.shape[0]
    devices = slots // 8
    circles = wide_ref.shape[0]

    spans = [(first, min(first + 2, items)) for first in range(0, items, 2)]


    def table_copy(i):
        return pltpu.make_async_copy(table_hbm.at[i], table_ref.at[i], table_sem.at[i])

    for i in range(3):
        table_copy(i).start()
    where = lax.broadcasted_iota(jnp.int32, (circle_half, slots), 0)
    pick_ref[...] = jnp.where(row_ref[...] == where, 1.0, 0.0).astype(jnp.bfloat16)
    for first, last in spans:
        natural = dot(pick_ref[...], coming_ref[:, first * width : last * width])
        for i in range(first, last):
            x = natural[:, (i - first) * width : (i - first + 1) * width].astype(jnp.bfloat16).T
            north, south = x[:half_width].astype(jnp.float32), x[half_width:].astype(jnp.float32)
            x_ref[i, :half_width] = (north + south).astype(jnp.bfloat16)
            x_ref[i, half_width:] = (north - south).astype(jnp.bfloat16)
    mark_rows(back_ref, order_ref[...].astype(jnp.float32))
    for t in range(circles):
        wide_ref[t, pl.ds(7, devices, stride=8), :] = jnp.zeros((devices, width), jnp.float32)

    for i in range(items):
        q = pair_ref[i]
        swap = (q % RADIX >= HALF).astype(jnp.int32)

        def weights(first, length):
            row = lax.broadcasted_iota(jnp.int32, (1, length), 1) + first
            second = row >= degrees - q
            degree = jnp.where(second, row - 1, q + row).astype(jnp.float32)
            damping = 1.0 / (1.0 + 4.0 * degree * (degree + 1.0) / float(degrees * degrees))
            wave = second.astype(jnp.int32) ^ swap
            parity = jnp.where(second, row + q, row) & 1
            code = 2 * parity + wave
            return [jnp.where(code == k, damping, 0.0) for k in range(4)]

        main_weights = weights(0, degrees)
        last_weights = weights(degrees, 1)
        table_copy(i).wait()
        if i + 3 < items:
            table_copy(i + 3).start()
        spectrum = dot(x_ref[i], table_ref[i, :degrees, :], NT)
        last_row = table_ref[i, degrees:, :].astype(jnp.float32)
        last = jnp.sum(x_ref[i].astype(jnp.float32) * last_row, axis=1, keepdims=True)
        scaled = jnp.concatenate(
            [
                (spectrum[k * quarter : (k + 1) * quarter] * main_weights[k]).astype(jnp.bfloat16)
                for k in range(4)
            ],
            axis=0,
        )
        scaled_last = jnp.concatenate(
            [
                (last[k * quarter : (k + 1) * quarter] * last_weights[k])
                .astype(jnp.bfloat16)
                .astype(jnp.float32)
                for k in range(4)
            ],
            axis=0,
        )
        total = dot(scaled, table_ref[i, :degrees, :])
        total = total + scaled_last * last_row
        even, odd = total[:half_width], total[half_width:]
        b_ref[i * width : i * width + half_width, :] = (even + odd).astype(jnp.bfloat16)
        b_ref[i * width + half_width : (i + 1) * width, :] = (even - odd).astype(jnp.bfloat16)

    for first, last in spans:
        moved = dot(back_ref[...], b_ref[first * width : last * width, :], NT)
        for i in range(first, last):
            for t in range(circles):
                wide_ref[t, pl.ds(i, devices, stride=8), :] = moved[
                    t * devices : (t + 1) * devices, (i - first) * width : (i - first + 1) * width
                ]
    copies = []
    for t in range(circles):
        send_ref[t] = wide_ref[t].astype(jnp.bfloat16)
        copy = pltpu.make_async_copy(
            send_ref.at[t], out_hbm.at[:, pl.ds(t * width, width)], out_sem.at[t]
        )
        copy.start()
        copies.append(copy)
    for copy in copies:
        copy.wait()


def synthesise_kernel(
    coming_ref,
    kappa_hbm,
    table_hbm,
    pair_ref,
    out_hbm,
    kappa_ref,
    table_ref,
    pick_ref,
    turned_ref,
    left_ref,
    u_ref,
    filt_ref,
    kappa_sem,
    table_sem,
    out_sem,
):
    rows = filt_ref.shape[1]
    circles = kappa_ref.shape[0]
    width = 8 * rows
    reps = pick_ref.shape[1]

    kappa_copy = pltpu.make_async_copy(kappa_hbm, kappa_ref, kappa_sem)
    kappa_copy.start()
    table_copy = pltpu.make_async_copy(table_hbm, table_ref, table_sem)
    table_copy.start()
    mark_rows(pick_ref, representative(pair_ref[...].astype(jnp.float32)))
    for t in range(circles):
        turned_ref[t * width : (t + 1) * width, :] = coming_ref[:, t * width : (t + 1) * width].T
    for first in range(0, HALF, 2):
        last = min(first + 2, HALF)
        coef = dot(turned_ref[...], pick_ref[:, first * WAVES : last * WAVES]).astype(jnp.bfloat16)
        for t in range(circles):
            for side in range(2):
                group = 2 * t + side
                for part in range(4):
                    base = t * width + side * 4 * rows + part * rows
                    for c in range(first, last):
                        left_ref[
                            c + part // 2,
                            group * rows : (group + 1) * rows,
                            part * WAVES : (part + 1) * WAVES,
                        ] = coef[base : base + rows, (c - first) * WAVES : (c - first + 1) * WAVES]
    table_copy.wait()
    two = 2 * WAVES
    for j in range(HALF + 1):
        if j == 0:
            u_ref[j, :, :BLOCK] = dot(left_ref[j, :, :two], table_ref[0, 0, :, :BLOCK])
        elif j == HALF:
            u_ref[j, :, :BLOCK] = dot(left_ref[j, :, two:], table_ref[1, j - 1, :, :BLOCK])
        else:
            u_ref[j] = dot(left_ref[j, :, :two], table_ref[0, j]) + dot(
                left_ref[j, :, two:], table_ref[1, j - 1]
            )
    kappa_copy.wait()

    def unfold(circle, side):
        group = 2 * circle + side
        at = pl.ds(pl.multiple_of(group * rows, rows), rows)
        for lane in range(0, BLOCK, 128):
            real = [u_ref[j, at, pl.ds(lane, 128)] for j in range(HALF + 1)]
            imag = [None] + [u_ref[j, at, pl.ds(BLOCK + lane, 128)] for j in range(1, HALF)]
            value = [None] * RADIX
            for b in range(4):
                cos_even = real[0]
                for j in (2, 4, 6):
                    cos_even = cos_even + real[j] * ring(j * b)[0]
                cos_odd = real[HALF] * ring(HALF * b)[0]
                for j in (1, 3, 5):
                    cos_odd = cos_odd + real[j] * ring(j * b)[0]
                if b == 0:
                    value[0] = cos_even + cos_odd
                    value[HALF] = cos_even - cos_odd
                    continue
                sin_even = imag[2] * ring(2 * b)[1]
                for j in (4, 6):
                    sin_even = sin_even + imag[j] * ring(j * b)[1]
                sin_odd = imag[1] * ring(b)[1]
                for j in (3, 5):
                    sin_odd = sin_odd + imag[j] * ring(j * b)[1]
                up, down = cos_even + cos_odd, cos_even - cos_odd
                sup, sdown = sin_even + sin_odd, sin_even - sin_odd
                value[b] = up - sup
                value[RADIX - b] = up + sup
                value[HALF + b] = down - sdown
                value[HALF - b] = down + sdown
            for b in range(RADIX):
                cut = pl.ds(b * BLOCK + lane, 128)
                scale = kappa_ref[circle, side : side + 1, cut]
                filt_ref[group, :, cut] = (value[b] * scale).astype(jnp.bfloat16)

    def out_copy(circle):
        return pltpu.make_async_copy(
            filt_ref.at[pl.ds(2 * circle, 2)], out_hbm.at[pl.ds(2 * circle, 2)], out_sem.at[circle]
        )

    def unfold_circle(circle, carry):
        unfold(circle, 0)
        unfold(circle, 1)
        out_copy(circle).start()
        return carry

    lax.fori_loop(0, circles, unfold_circle, 0)
    for t in range(circles):
        out_copy(t).wait()


VMEM = pl.BlockSpec(memory_space=pltpu.VMEM)
SMEM = pl.BlockSpec(memory_space=pltpu.SMEM)
ANY = pl.BlockSpec(memory_space=pl.ANY)
HBM = pl.BlockSpec(memory_space=pltpu.HBM)
NOWHERE = 10000


def stay(array):
    return pltpu.with_memory_space_constraint(array, pltpu.HBM)


def near(array):
    return pltpu.with_memory_space_constraint(array, pltpu.VMEM)


def limit(mib):
    return pltpu.CompilerParams(vmem_limit_bytes=mib * 2**20)


def per_device(probe_field, kappa_field, circle_order, pair_order, legendre_table):
    circles, sides, probes, longitudes = probe_field.shape
    items, row_count, circle_half = legendre_table.shape
    devices = lax.axis_size(AXES)
    groups = circles * sides
    reps = HALF * WAVES
    width = 8 * probes
    slots = devices * 8
    ahead, back = fourier_tables(longitudes)
    ahead, back = jnp.asarray(ahead), jnp.asarray(back)

    def by_device(order, count):
        held = order.reshape(devices, count)
        return jnp.pad(held, ((0, 0), (0, 8 - count)), constant_values=NOWHERE).reshape(1, slots)

    def by_place(order, count):
        return order.reshape(devices, count).T.reshape(1, count * devices)

    def swap_over(payload):
        blocks = payload.reshape(devices, 8, payload.shape[1])
        moved = lax.all_to_all(blocks, AXES, split_axis=0, concat_axis=0, tiled=True)
        return moved.reshape(payload.shape)

    bf16, f32 = jnp.bfloat16, jnp.float32
    dma = pltpu.SemaphoreType.DMA
    sending = pl.pallas_call(
        analyse_kernel,
        out_shape=pltpu.HBM((slots, items * width), bf16),
        in_specs=[HBM, HBM, HBM, VMEM],
        out_specs=HBM,
        scratch_shapes=[
            pltpu.VMEM((groups, probes, longitudes), bf16),
            pltpu.VMEM(kappa_field.shape, f32),
            pltpu.VMEM(ahead.shape, bf16),
            pltpu.VMEM((HALF + 1, groups * probes, 2 * BLOCK), bf16),
            pltpu.VMEM((circles * width, reps), bf16),
            pltpu.VMEM((items * devices, reps), bf16),
            pltpu.VMEM((items, slots, width), f32),
            pltpu.VMEM((items, slots, width), bf16),
            pltpu.VMEM((items * devices, WAVES), f32),
            dma((circles,)),
            dma,
            dma((2,)),
            dma((items,)),
        ],
        compiler_params=limit(40),
        name="analyse",
    )(
        stay(probe_field.reshape(groups, probes, longitudes)),
        stay(kappa_field),
        stay(ahead),
        pair_order.reshape(items, devices),
    )
    coming = swap_over(sending)

    pairs = lax.dynamic_slice(pair_order, (lax.axis_index(AXES) * items,), (items,))
    sending = pl.pallas_call(
        legendre_kernel,
        out_shape=pltpu.HBM((slots, circles * width), bf16),
        in_specs=[SMEM, VMEM, HBM, VMEM, VMEM],
        out_specs=HBM,
        scratch_shapes=[
            pltpu.VMEM((items, row_count, circle_half), bf16),
            pltpu.VMEM((items, width, circle_half), bf16),
            pltpu.VMEM((items * width, circle_half), bf16),
            pltpu.VMEM((circle_half, slots), bf16),
            pltpu.VMEM((circles * devices, circle_half), bf16),
            pltpu.VMEM((circles, slots, width), f32),
            pltpu.VMEM((circles, slots, width), bf16),
            dma((items,)),
            dma((circles,)),
        ],
        compiler_params=limit(48),
        name="legendre",
    )(
        pairs,
        near(coming),
        stay(legendre_table),
        by_device(circle_order, circles),
        by_place(circle_order, circles),
    )
    coming = swap_over(sending)

    filtered = pl.pallas_call(
        synthesise_kernel,
        out_shape=jax.ShapeDtypeStruct((groups, probes, longitudes), bf16),
        in_specs=[VMEM, HBM, HBM, VMEM],
        out_specs=HBM,
        scratch_shapes=[
            pltpu.VMEM(kappa_field.shape, f32),
            pltpu.VMEM(back.shape, bf16),
            pltpu.VMEM((slots, reps), bf16),
            pltpu.VMEM((circles * width, slots), bf16),
            pltpu.VMEM((HALF + 1, groups * probes, 4 * WAVES), bf16),
            pltpu.VMEM((HALF + 1, groups * probes, 2 * BLOCK), f32),
            pltpu.VMEM((groups, probes, longitudes), bf16),
            dma,
            dma,
            dma((circles,)),
        ],
        compiler_params=limit(40),
        name="synthesise",
    )(
        near(coming), stay(kappa_field), stay(back), by_device(pair_order, items)
    )
    return filtered.reshape(circles, sides, probes, longitudes)


def solution(mesh):
    return jax.shard_map(
        per_device,
        mesh=mesh,
        in_specs=(
            P(AXES, None, None, None),
            P(AXES, None, None),
            P(),
            P(),
            P(AXES, None, None),
        ),
        out_specs=P(AXES, None, None, None),
        check_vma=False,
    )
```
